256 devices in a mesh: dp: 16 (over z, x_hi), region: 16 (over y, x_lo, core).
Axes of the slice: x: 4 (x_hi: 2, x_lo: 2; x = x_hi * 2 + x_lo), y: 4, z: 8, core: 2. Of those that a mesh axis runs over, the one named last changes fastest.
Arguments:
- ensemble: float32 [200, 262144], P(None, ('dp', 'region')), may hold values from -6 to 6
- predicted: bfloat16 [200, 393216], P(None, ('dp', 'region')), may hold values from -6 to 6
- innovation: bfloat16 [200, 393216], P(None, ('dp', 'region')), may hold values from -0.29882812 to 0.29882812
- taper_level: int32 [256, 512], replicated, may hold values from 0 to 4
- slot_order: int32 [16, 32], P('dp'), may hold values from 0 to 31, each once within a row
Outputs:
- increment: float32 [200, 262144], P(None, ('dp', 'region'))
The draws below stay inside these ranges and needn't reach their ends.
Inputs may be any that keep to these rules, and one draw needn't show every extreme that they name: `slot_order`: each row is a permutation.
All inputs are finite; a program needn't handle non-finite values.
Results may differ from the reference program's by a relative error of at most 0.0003.
Values may be sent and summed in bfloat16 or wider, within the bound.
No kernel may reach another device: no remote copies, remote signals or barrier semaphores. Data moves between devices by JAX's collectives and lax.ppermute only.
A program may use at most 128 MiB of HBM per device.

```python
import jax
import jax.numpy as jnp
from jax import lax

NE = 200
NDB = 1536
RC = 512
LEVELS = 4
NR_BLK = 32
NCELLS = 262144
REGIONS = 512
DBLOCKS = 256
NDATA = 393216
N_DP = 16


def touch_ends(result, own_key, smallest, high):
    index_at = [jax.random.randint(jax.random.fold_in(own_key, axis), (), 0, length) for axis, length in enumerate(result.shape)]
    widest = result.shape.index(max(result.shape))
    neighbour = index_at[:widest] + [(index_at[widest] + 1) % result.shape[widest]] + index_at[widest + 1:]
    return result.at[tuple(index_at)].set(smallest).at[tuple(neighbour)].set(high)


def steps_of(stream_key, extent, shards, least, largest):
    gain, own = 1.0, jax.random.fold_in(stream_key, 6)
    for position, blocks in shards:
        heights = jnp.exp(jax.random.uniform(jax.random.fold_in(own, position), (blocks,), jnp.float32, least / len(shards), largest / len(shards)))
        gain = gain * jnp.repeat(heights, extent[position] // blocks).reshape([-1 if axis == position else 1 for axis in range(len(extent))])
    return gain


def scatter_about(key, dims, deviation, bound, shards=(), held_as=jnp.bfloat16):
    values = jax.random.normal(key, dims, jnp.float32) * deviation
    if len(shards) > 0:
        values = steps_of(key, dims, shards, -0.22, 0.18) * values
    return jnp.clip(values, min=-bound, max=bound).astype(held_as)


def setup_inputs(seed: int = 0) -> dict:
    seeds = jax.random.split(jax.random.key(seed), 6)
    ensemble = scatter_about(seeds[0], (NE, NCELLS), 1.0, 6.0, ((1, 256),), jnp.float32)
    predicted = scatter_about(seeds[1], (NE, NDATA), 1.0, 6.0, ((1, 256),))
    innovation = scatter_about(seeds[2], (NE, NDATA), 0.05, 0.29882812, ((1, 256),))
    taper_level = touch_ends(jax.random.randint(seeds[3], (DBLOCKS, REGIONS), 0, LEVELS + 1), jax.random.fold_in(seeds[3], 1), 0, LEVELS).astype(jnp.int32)
    slot_order = jax.vmap(lambda own: jax.random.permutation(own, NR_BLK))(jax.random.split(seeds[4], N_DP)).reshape((N_DP, NR_BLK)).astype(jnp.int32)
    return {"ensemble": ensemble, "predicted": predicted, "innovation": innovation, "taper_level": taper_level, "slot_order": slot_order}


def taper_table():
    values = []
    for level in range(LEVELS + 1):
        z = 2.0 * (LEVELS - level) / LEVELS
        if z <= 1.0:
            value = -z ** 5 / 4.0 + z ** 4 / 2.0 + 5.0 * z ** 3 / 8.0 - 5.0 * z ** 2 / 3.0 + 1.0
        else:
            value = z ** 5 / 12.0 - z ** 4 / 2.0 + 5.0 * z ** 3 / 8.0 + 5.0 * z ** 2 / 3.0 - 5.0 * z + 4.0 - 2.0 / (3.0 * z)
        values.append(max(value, 0.0))
    return values


def taper_weights(levels_in):
    table = taper_table()
    total = jnp.zeros(levels_in.shape, jnp.float32)
    for level in range(LEVELS + 1):
        total = total + jnp.float32(table[level]) * (levels_in == level).astype(jnp.float32)
    return total


def reference(ensemble, predicted, innovation, taper_level, slot_order):
    anomaly = ensemble - jnp.mean(ensemble, axis=0, keepdims=True)
    y_blocks = predicted.astype(jnp.float32).reshape(NE, DBLOCKS, NDB)
    w_blocks = innovation.astype(jnp.float32).reshape(NE, DBLOCKS, NDB)
    block_gain = jnp.einsum("ebd,fbd->bef", y_blocks, w_blocks, precision=lax.Precision.HIGHEST)
    taper = taper_weights(taper_level)
    region_gain = jnp.einsum("br,bef->ref", taper, block_gain, precision=lax.Precision.HIGHEST)
    cells = anomaly.reshape(NE, REGIONS, RC)
    local = jnp.einsum("ref,erc->frc", region_gain, cells, precision=lax.Precision.HIGHEST) / (NE - 1.0)
    inverse = jnp.argsort(slot_order, axis=1).astype(jnp.int32)
    offsets = (jnp.arange(N_DP, dtype=jnp.int32) * NR_BLK)[:, None]
    picked = (inverse + offsets).reshape(-1)
    increment = jnp.take(local, picked, axis=1)
    return increment.reshape(NE, NCELLS)
```

```python
import jax
import jax.numpy as jnp
from jax import lax
from jax.experimental import pallas as pl
from jax.experimental.pallas import tpu as pltpu
from jax.sharding import PartitionSpec as P

LEVELS = 4
LANES = 128
HIGHEST = lax.Precision.HIGHEST
BOTH = ("dp", "region")


def taper_table(levels):
    values = []
    for level in range(levels + 1):
        z = 2.0 * (levels - level) / levels
        if z <= 1.0:
            value = -(z**5) / 4.0 + z**4 / 2.0 + 5.0 * z**3 / 8.0 - 5.0 * z**2 / 3.0 + 1.0
        else:
            value = (
                z**5 / 12.0
                - z**4 / 2.0
                + 5.0 * z**3 / 8.0
                + 5.0 * z**2 / 3.0
                - 5.0 * z
                + 4.0
                - 2.0 / (3.0 * z)
            )
        values.append(max(value, 0.0))
    return values


TABLE = taper_table(LEVELS)

PLANE = 32
GAIN = 7
ROWS = 16
COLS = 2 * GAIN * LANES
UNITS = 7
TILES = 4


def gain_rows(k):
    return slice(k * ROWS // 2, k * ROWS // 2 + GAIN)


def block_kernel(y_ref, w_ref, slot_ref, out_ref, gain):
    members = y_ref.shape[0]
    gain[...] = jnp.zeros_like(gain)
    gain[0:members, 0:members] = lax.dot_general(
        y_ref[...], w_ref[...], (((1,), (1,)), ((), ())), preferred_element_type=jnp.float32
    )
    blocks = slot_ref.shape[1]
    row = lax.broadcasted_iota(jnp.int32, (blocks, LANES), 0)
    lane = lax.broadcasted_iota(jnp.int32, (blocks, LANES), 1)
    place = (lane == row + (members - LANES)).astype(jnp.float32)
    order = jnp.broadcast_to(slot_ref[...].astype(jnp.float32), (8, blocks))
    order = lax.dot_general(
        order, place, (((1,), (0,)), ((), ())), preferred_element_type=jnp.float32
    )
    lanes = lax.broadcasted_iota(jnp.int32, (gain.shape[0], LANES), 1)
    spread = jnp.broadcast_to(order[0:1, :], (gain.shape[0], LANES))
    gain[:, LANES:] = jnp.where(lanes >= members - LANES, spread, gain[:, LANES:])
    for a in range(PLANE):
        for k in range(2):
            out_ref[a, gain_rows(k), :] = gain[
                a * GAIN : (a + 1) * GAIN, k * LANES : (k + 1) * LANES
            ]


def turn_kernel(got_ref, out_ref):
    for k in range(2):
        for g in range(GAIN):
            column = (k * GAIN + g) * LANES
            out_ref[:, column : column + LANES] = got_ref[
                pl.ds(k * ROWS // 2 + g, PLANE, stride=ROWS), :
            ]


def spread_kernel(ens_ref, out_ref):
    members = ens_ref.shape[0]
    for u in range(members // 8 * TILES):
        t, l = u // TILES, u % TILES
        for k in range(2):
            first = (k * TILES + l) * LANES
            out_ref[u // UNITS, k, u % UNITS * 8 : u % UNITS * 8 + 8, :] = ens_ref[
                t * 8 : t * 8 + 8, first : first + LANES
            ]


def slot_kernel(slot_ref, got_ref, out_ref):
    for r in range(slot_ref.shape[1]):
        out_ref[pl.ds(slot_ref[0, r], 1)] = got_ref[r : r + 1]


def gain_kernel(slot_ref, x_ref, level_ref, out_ref, sorted_level):
    regions = level_ref.shape[0]
    blocks = slot_ref.shape[1]
    for r in range(regions):
        dest = (r // blocks) * blocks + slot_ref[r // blocks, r % blocks]
        sorted_level[pl.ds(dest, 1), :] = level_ref[r : r + 1, :]
    level = sorted_level[...]
    taper = jnp.zeros(level.shape, jnp.float32)
    for value in range(LEVELS + 1):
        taper = jnp.where(level == value, jnp.float32(TABLE[value]), taper)
    region_gain = lax.dot_general(
        taper,
        x_ref[...],
        (((1,), (0,)), ((), ())),
        precision=HIGHEST,
        preferred_element_type=jnp.float32,
    )
    for k in range(2):
        for g in range(GAIN):
            column = (k * GAIN + g) * LANES
            out_ref[pl.ds(k * ROWS // 2 + g, regions, stride=ROWS), :] = region_gain[
                :, column : column + LANES
            ]


def update_kernel(gain_ref, ens_ref, out_ref, cells, gain):
    members = out_ref.shape[0]
    for s in range(2):
        for u in range(members // 8 * TILES):
            t, l = u // TILES, u % TILES
            cells[t * 8 : t * 8 + 8, l * LANES : (l + 1) * LANES] = ens_ref[
                u // UNITS, s, u % UNITS * 8 : u % UNITS * 8 + 8, :
            ]
        for a in range(-(-members // GAIN)):
            for k in range(2):
                gain[a * GAIN : (a + 1) * GAIN, k * LANES : (k + 1) * LANES] = gain_ref[
                    a, s, gain_rows(k), :
                ]
        values = cells[...]
        anomaly = values - jnp.mean(values, axis=0, keepdims=True)
        local = lax.dot_general(
            gain[0:members, :],
            anomaly,
            (((0,), (0,)), ((), ())),
            precision=HIGHEST,
            preferred_element_type=jnp.float32,
        )
        out_ref[:, s * TILES * LANES : (s + 1) * TILES * LANES] = local[
            0:members, :
        ] * jnp.float32(1.0 / (members - 1.0))


VMEM = pl.BlockSpec(memory_space=pltpu.VMEM)
SMEM = pl.BlockSpec(memory_space=pltpu.SMEM)


def call(kernel, shape, in_specs, scratch=()):
    return pl.pallas_call(
        kernel,
        out_shape=jax.ShapeDtypeStruct(shape, jnp.float32),
        in_specs=in_specs,
        out_specs=VMEM,
        scratch_shapes=list(scratch),
        compiler_params=pltpu.CompilerParams(vmem_limit_bytes=40 * 1024 * 1024),
    )


def per_device(ensemble, predicted, innovation, taper_level, slot_order):
    members = ensemble.shape[0]
    blocks = slot_order.shape[1]
    data_blocks = taper_level.shape[0]
    dp_count = lax.axis_size("dp")
    planes = data_blocks // PLANE
    plane_groups = [[z * PLANE + a for a in range(PLANE)] for z in range(planes)]
    z_groups = [[2 * z + h for z in range(planes)] for h in range(dp_count // planes)]
    z = lax.axis_index("dp") // 2
    level = lax.dynamic_slice_in_dim(taper_level, z * 2 * blocks, 2 * blocks, 1).T

    sent = call(
        block_kernel,
        (PLANE, ROWS, LANES),
        [VMEM] * 3,
        [pltpu.VMEM((PLANE * GAIN, 2 * LANES), jnp.float32)],
    )(predicted, innovation, slot_order)
    got = lax.all_to_all(
        sent, BOTH, split_axis=0, concat_axis=0, tiled=True, axis_index_groups=plane_groups
    )
    slots = got[:: PLANE // 2, ROWS // 2, members - LANES : members - LANES + blocks]
    mine = call(turn_kernel, (PLANE, COLS), [VMEM])(got.reshape(PLANE * ROWS, LANES))
    gains = lax.all_gather(mine, "dp", axis=0, tiled=True, axis_index_groups=z_groups)

    group = lax.axis_size("region")
    wide = UNITS * 8
    ens = call(spread_kernel, (group, 2, wide, LANES), [VMEM])(ensemble)
    ens, _ = lax.optimization_barrier((ens, mine))
    ens = lax.all_to_all(ens, "region", split_axis=0, concat_axis=0, tiled=True)
    ens = call(slot_kernel, (blocks, wide, LANES), [SMEM, VMEM])(
        slot_order, ens.reshape(blocks, wide, LANES)
    )
    ens = lax.all_to_all(
        ens.reshape(group, 2, wide, LANES), "region", split_axis=0, concat_axis=0, tiled=True
    )

    back = call(
        gain_kernel,
        (2 * blocks * ROWS, LANES),
        [SMEM, VMEM, VMEM],
        [pltpu.VMEM((2 * blocks, data_blocks), jnp.int32)],
    )(slots.astype(jnp.int32), gains, level)
    arrived = lax.all_to_all(
        back.reshape(PLANE, 2, ROWS, LANES),
        BOTH,
        split_axis=0,
        concat_axis=0,
        tiled=True,
        axis_index_groups=plane_groups,
    )
    return call(
        update_kernel,
        ensemble.shape,
        [VMEM] * 2,
        [
            pltpu.VMEM((members, TILES * LANES), jnp.float32),
            pltpu.VMEM((PLANE * GAIN, 2 * LANES), jnp.float32),
        ],
    )(arrived, ens)


def solution(mesh):
    return jax.shard_map(
        per_device,
        mesh=mesh,
        in_specs=(
            P(None, BOTH),
            P(None, BOTH),
            P(None, BOTH),
            P(),
            P("dp", None),
        ),
        out_specs=P(None, BOTH),
        check_vma=False,
    )
```

```python
import jax
import jax.numpy as jnp
from jax import lax
from jax.experimental import pallas as pl
from jax.experimental.pallas import tpu as pltpu
from jax.sharding import PartitionSpec as P

LEVELS = 4
LANES = 128
HIGHEST = lax.Precision.HIGHEST
BOTH = ("dp", "region")


def taper_table(levels):
    values = []
    for level in range(levels + 1):
        z = 2.0 * (levels - level) / levels
        if z <= 1.0:
            value = -(z**5) / 4.0 + z**4 / 2.0 + 5.0 * z**3 / 8.0 - 5.0 * z**2 / 3.0 + 1.0
        else:
            value = (
                z**5 / 12.0
                - z**4 / 2.0
                + 5.0 * z**3 / 8.0
                + 5.0 * z**2 / 3.0
                - 5.0 * z
                + 4.0
                - 2.0 / (3.0 * z)
            )
        values.append(max(value, 0.0))
    return values


TABLE = taper_table(LEVELS)

SLAB = 64
SHARE = 5
PIECE = 13
HALF = 16
SENT = 2 * HALF
BACK = 40
TILES = 4
WIDTH = 25
SETS = 5
GROUPS = 8
RUN = GROUPS * SHARE


def lane_of(rows):
    return lax.broadcasted_iota(jnp.int32, (rows, LANES), 1)


def sent_rows(j):
    return HALF - 3 + j if j < 3 else SENT - 6 + j


def back_rows(t, j):
    return t * HALF + PIECE + j if j < 3 else SENT + 2 * t + j - 3


def pieces(members):
    count = SLAB // TILES
    for d in range(SLAB):
        first = d % count * PIECE
        yield d, d // count, first, min(PIECE, members - first)


def pack_kernel(y_ref, w_ref, ens_ref, slot_ref, out_ref, gain, packed, order):
    members = ens_ref.shape[0]
    gain[:, 0:members] = lax.dot_general(
        y_ref[...], w_ref[...], (((1,), (1,)), ((), ())), preferred_element_type=jnp.float32
    )
    for d, tile, first, rows in pieces(members):
        for k in range(2):
            column = (k * TILES + tile) * LANES
            out_ref[d, k * HALF : k * HALF + rows, :] = ens_ref[
                first : first + rows, column : column + LANES
            ]
    order[:, 0 : slot_ref.shape[1]] = slot_ref[...].astype(jnp.float32)
    lane = lane_of(RUN)
    for f in range(GROUPS):
        total = None
        for g in range(SETS):
            low = gain[g * RUN : (g + 1) * RUN, 0:LANES]
            high = gain[g * RUN : (g + 1) * RUN, LANES : 2 * LANES]
            start, end = f * WIDTH, (f + 1) * WIDTH
            if end <= LANES:
                part = low
            elif start >= LANES:
                part = high
            else:
                part = jnp.where(lane >= start, low, high)
            part = pltpu.roll(part, (g - f) * WIDTH % LANES, 1)
            total = part if total is None else jnp.where(lane >= g * WIDTH, part, total)
        packed[f * RUN : (f + 1) * RUN, :] = total
    for d in range(SLAB):
        first = d * SHARE
        out_ref[d, sent_rows(0) : sent_rows(0) + 3, :] = packed[first : first + 3, :]
        out_ref[d, sent_rows(3) : sent_rows(3) + 2, :] = packed[first + 3 : first + 5, :]
        out_ref[d, SENT - 1 : SENT, :] = order[...]


def turn_kernel(got_ref, out_ref):
    for j in range(SHARE):
        out_ref[:, j * LANES : (j + 1) * LANES] = got_ref[
            pl.ds(sent_rows(j), SLAB, stride=SENT), :
        ]


def sort_kernel(slot_ref, level_ref, got_ref, taper_ref, out_ref, level):
    regions = level_ref.shape[0]
    blocks = slot_ref.shape[1]
    for r in range(regions):
        dest = r // blocks * blocks + slot_ref[r // blocks, r % blocks]
        owner, t = lax.div(dest, 2), lax.rem(dest, 2)
        level[pl.ds(t * SLAB + owner, 1), :] = level_ref[r : r + 1, :]
        out_ref[pl.ds(pl.multiple_of(owner * BACK + t * HALF, 8), HALF), :] = got_ref[
            r * HALF : (r + 1) * HALF, :
        ]
    levels = level[...]
    taper = jnp.zeros(levels.shape, jnp.float32)
    for value in range(LEVELS + 1):
        taper = jnp.where(levels == value, jnp.float32(TABLE[value]), taper)
    taper_ref[...] = taper


def gain_kernel(taper_ref, x0_ref, x1_ref, x2_ref, x3_ref, x4_ref, back_ref, out_ref):
    del back_ref
    taper = taper_ref[...]
    far = jnp.concatenate([x3_ref[...], x4_ref[...]], axis=0)
    total = None
    for i, x in enumerate((x0_ref[...], x1_ref[...], x2_ref[...], far)):
        part = lax.dot_general(
            taper[:, i * SLAB : (i + 1) * SLAB],
            x,
            (((1,), (0,)), ((), ())),
            precision=HIGHEST,
            preferred_element_type=jnp.float32,
        )
        total = part if total is None else total + part
    for t in range(2):
        for j in range(SHARE):
            out_ref[pl.ds(back_rows(t, j), SLAB, stride=BACK), :] = total[
                t * SLAB : (t + 1) * SLAB, j * LANES : (j + 1) * LANES
            ]


def update_kernel(got_ref, out_ref, cells, packed, gain):
    members = out_ref.shape[0]
    lane = lane_of(RUN)
    for t in range(2):
        for d, tile, first, rows in pieces(members):
            cells[first : first + rows, tile * LANES : (tile + 1) * LANES] = got_ref[
                d, t * HALF : t * HALF + rows, :
            ]
        for d in range(SLAB):
            near, rest = back_rows(t, 0), back_rows(t, 3)
            packed[d * SHARE : d * SHARE + 3, :] = got_ref[d, near : near + 3, :]
            packed[d * SHARE + 3 : d * SHARE + 5, :] = got_ref[d, rest : rest + 2, :]
        for g in range(SETS):
            halves = [None, None]
            for f in range(GROUPS):
                part = pltpu.roll(packed[f * RUN : (f + 1) * RUN, :], (f - g) * WIDTH % LANES, 1)
                for h in range(2):
                    start = f * WIDTH - h * LANES
                    if start < LANES and start + WIDTH > 0:
                        halves[h] = (
                            part if halves[h] is None else jnp.where(lane >= start, part, halves[h])
                        )
            for h in range(2):
                gain[g * RUN : (g + 1) * RUN, h * LANES : (h + 1) * LANES] = halves[h]
        values = cells[...]
        anomaly = values - jnp.mean(values, axis=0, keepdims=True)
        local = lax.dot_general(
            gain[...],
            anomaly,
            (((0,), (0,)), ((), ())),
            precision=HIGHEST,
            preferred_element_type=jnp.float32,
        )
        out_ref[:, t * TILES * LANES : (t + 1) * TILES * LANES] = local[
            0:members, :
        ] * jnp.float32(1.0 / (members - 1.0))


VMEM = pl.BlockSpec(memory_space=pltpu.VMEM)
SMEM = pl.BlockSpec(memory_space=pltpu.SMEM)


def call(kernel, shapes, in_specs, scratch=(), aliases=None):
    many = isinstance(shapes, list)
    outs = [jax.ShapeDtypeStruct(shape, jnp.float32) for shape in (shapes if many else [shapes])]
    return pl.pallas_call(
        kernel,
        out_shape=outs if many else outs[0],
        in_specs=in_specs,
        out_specs=[VMEM] * len(outs) if many else VMEM,
        scratch_shapes=list(scratch),
        input_output_aliases=aliases or {},
        compiler_params=pltpu.CompilerParams(vmem_limit_bytes=40 * 1024 * 1024),
    )


def scratch(rows, columns, dtype=jnp.float32):
    return pltpu.VMEM((rows, columns), dtype)


def per_device(ensemble, predicted, innovation, taper_level, slot_order):
    members = ensemble.shape[0]
    blocks = slot_order.shape[1]
    data_blocks = taper_level.shape[0]
    slabs = data_blocks // SLAB
    regions = 2 * SLAB
    groups = [[s * SLAB + a for a in range(SLAB)] for s in range(slabs)]
    slab = lax.axis_index(BOTH) // SLAB

    def shift(x, by):
        pairs = [
            (s * SLAB + a, (s + by) % slabs * SLAB + a) for s in range(slabs) for a in range(SLAB)
        ]
        return lax.ppermute(x, BOTH, pairs)

    def exchange(x):
        return lax.all_to_all(
            x, BOTH, split_axis=0, concat_axis=0, tiled=True, axis_index_groups=groups
        )

    columns = lax.dynamic_slice_in_dim(taper_level, slab * regions, regions, 1)
    level = jnp.concatenate(
        [
            lax.dynamic_slice_in_dim(columns, (slab + by) % slabs * SLAB, SLAB, 0)
            for by in (0, -1, 1, 2)
        ],
        axis=0,
    ).T

    sent = call(
        pack_kernel,
        (SLAB, SENT, LANES),
        [VMEM] * 4,
        [scratch(members, 2 * LANES), scratch(GROUPS * RUN, LANES), scratch(1, LANES)],
    )(predicted, innovation, ensemble, slot_order)
    got = exchange(sent)
    flat = got.reshape(SLAB * SENT, LANES)
    slots = got[:: SLAB // 4, SENT - 1, 0:blocks].astype(jnp.int32)

    x0 = call(turn_kernel, (SLAB, SHARE * LANES), [VMEM])(flat)
    x1 = shift(x0, 1)
    x2 = shift(x0, -1)
    x3 = shift(x1[: SLAB // 2], 1)
    x4 = shift(x2[SLAB // 2 :], -1)
    taper, back = call(
        sort_kernel,
        [(regions, data_blocks), (SLAB * BACK, LANES)],
        [SMEM, VMEM, VMEM],
        [scratch(regions, data_blocks, jnp.int32)],
    )(slots, level, flat)
    back = call(gain_kernel, (SLAB * BACK, LANES), [VMEM] * 7, aliases={6: 0})(
        taper, x0, x1, x2, x3, x4, back
    )
    arrived = exchange(back.reshape(SLAB, BACK, LANES))
    return call(
        update_kernel,
        ensemble.shape,
        [VMEM],
        [
            scratch(members, TILES * LANES),
            scratch(GROUPS * RUN, LANES),
            scratch(members, 2 * LANES),
        ],
    )(arrived)


def solution(mesh):
    return jax.shard_map(
        per_device,
        mesh=mesh,
        in_specs=(
            P(None, BOTH),
            P(None, BOTH),
            P(None, BOTH),
            P(),
            P("dp", None),
        ),
        out_specs=P(None, BOTH),
        check_vma=False,
    )
```

```python
import jax
import jax.numpy as jnp
from jax import lax
from jax.experimental import pallas as pl
from jax.experimental.pallas import tpu as pltpu
from jax.sharding import PartitionSpec as P

LEVELS = 4
LANES = 128
HIGHEST = lax.Precision.HIGHEST
BOTH = ("dp", "region")


def taper_table(levels):
    values = []
    for level in range(levels + 1):
        z = 2.0 * (levels - level) / levels
        if z <= 1.0:
            value = -(z**5) / 4.0 + z**4 / 2.0 + 5.0 * z**3 / 8.0 - 5.0 * z**2 / 3.0 + 1.0
        else:
            value = (
                z**5 / 12.0
                - z**4 / 2.0
                + 5.0 * z**3 / 8.0
                + 5.0 * z**2 / 3.0
                - 5.0 * z
                + 4.0
                - 2.0 / (3.0 * z)
            )
        values.append(max(value, 0.0))
    return values


TABLE = taper_table(LEVELS)

SLAB = 64
SHARE = 5
PIECE = 13
HALF = 16
SENT = 2 * HALF
BACK = 40
TILES = 4
WIDTH = 25
SETS = 5
GROUPS = 8
CUTS = 3
RUN = GROUPS * SHARE


def lane_of(rows):
    return lax.broadcasted_iota(jnp.int32, (rows, LANES), 1)


def sent_rows(j):
    return HALF - 3 + j if j < 3 else SENT - 6 + j


def back_rows(t, j):
    return t * HALF + PIECE + j if j < 3 else SENT + 2 * t + j - 3


def pieces(members):
    count = SLAB // TILES
    for d in range(SLAB):
        first = d % count * PIECE
        yield d, d // count, first, min(PIECE, members - first)


def pack_kernel(
    y_hbm,
    w_hbm,
    ens_hbm,
    slot_hbm,
    out_ref,
    gain,
    packed,
    order,
    y_ref,
    w_ref,
    ens_ref,
    slot_ref,
    sems,
):
    members = ens_ref.shape[0]
    step = y_ref.shape[1] // CUTS
    cuts = [pl.ds(i * step, step) for i in range(CUTS)]
    copies = [
        [
            pltpu.make_async_copy(hbm.at[:, cut], ref.at[:, cut], sems.at[k, i])
            for k, (hbm, ref) in enumerate(((y_hbm, y_ref), (w_hbm, w_ref)))
        ]
        for i, cut in enumerate(cuts)
    ]
    wide = ens_ref.shape[1] // 2
    halves = [pl.ds(k * wide, wide) for k in range(2)]
    ens_copies = [
        pltpu.make_async_copy(ens_hbm.at[:, half], ens_ref.at[:, half], sems.at[2, k])
        for k, half in enumerate(halves)
    ]
    for pair in copies:
        for copy in pair:
            copy.start()
    ens_copies.append(pltpu.make_async_copy(slot_hbm, slot_ref, sems.at[2, 2]))
    for copy in ens_copies:
        copy.start()
    total = None
    for cut, pair in zip(cuts, copies):
        for copy in pair:
            copy.wait()
        part = lax.dot_general(
            y_ref[:, cut],
            w_ref[:, cut],
            (((1,), (1,)), ((), ())),
            preferred_element_type=jnp.float32,
        )
        total = part if total is None else total + part
    gain[:, 0:members] = total
    for copy in ens_copies:
        copy.wait()
    for d, tile, first, rows in pieces(members):
        for k in range(2):
            column = (k * TILES + tile) * LANES
            out_ref[d, k * HALF : k * HALF + rows, :] = ens_ref[
                first : first + rows, column : column + LANES
            ]
    order[:, 0 : slot_ref.shape[1]] = slot_ref[...].astype(jnp.float32)
    lane = lane_of(RUN)
    for f in range(GROUPS):
        total = None
        for g in range(SETS):
            low = gain[g * RUN : (g + 1) * RUN, 0:LANES]
            high = gain[g * RUN : (g + 1) * RUN, LANES : 2 * LANES]
            start, end = f * WIDTH, (f + 1) * WIDTH
            if end <= LANES:
                part = low
            elif start >= LANES:
                part = high
            else:
                part = jnp.where(lane >= start, low, high)
            part = pltpu.roll(part, (g - f) * WIDTH % LANES, 1)
            total = part if total is None else jnp.where(lane >= g * WIDTH, part, total)
        packed[f * RUN : (f + 1) * RUN, :] = total
    for d in range(SLAB):
        first = d * SHARE
        out_ref[d, sent_rows(0) : sent_rows(0) + 3, :] = packed[first : first + 3, :]
        out_ref[d, sent_rows(3) : sent_rows(3) + 2, :] = packed[first + 3 : first + 5, :]
        out_ref[d, SENT - 1 : SENT, :] = order[...]


def turn_kernel(got_ref, out_ref):
    for j in range(SHARE):
        out_ref[:, j * LANES : (j + 1) * LANES] = got_ref[
            pl.ds(sent_rows(j), SLAB, stride=SENT), :
        ]


def sort_kernel(slot_ref, level_ref, got_ref, taper_ref, out_ref, level):
    regions = level_ref.shape[0]
    blocks = slot_ref.shape[1]
    for r in range(regions):
        dest = r // blocks * blocks + slot_ref[r // blocks, r % blocks]
        owner, t = lax.div(dest, 2), lax.rem(dest, 2)
        level[pl.ds(t * SLAB + owner, 1), :] = level_ref[r : r + 1, :]
        out_ref[pl.ds(pl.multiple_of(owner * BACK + t * HALF, 8), HALF), :] = got_ref[
            r * HALF : (r + 1) * HALF, :
        ]
    levels = level[...]
    taper = jnp.zeros(levels.shape, jnp.float32)
    for value in range(LEVELS + 1):
        taper = jnp.where(levels == value, jnp.float32(TABLE[value]), taper)
    taper_ref[...] = taper


def weigh(taper, first, refs):
    total = None
    for ref in refs:
        rows = ref.shape[0]
        part = lax.dot_general(
            taper[:, first : first + rows],
            ref[...],
            (((1,), (0,)), ((), ())),
            precision=HIGHEST,
            preferred_element_type=jnp.float32,
        )
        total = part if total is None else total + part
        first += rows
    return total


def near_kernel(taper_ref, *refs):
    refs[-1][...] = weigh(taper_ref[...], 0, refs[:-1])


def far_kernel(taper_ref, near_ref, *refs):
    out_ref = refs[-1]
    far = refs[:-2]
    held = sum(ref.shape[0] for ref in far)
    total = near_ref[...] + weigh(taper_ref[...], taper_ref.shape[1] - held, far)
    for t in range(2):
        for j in range(SHARE):
            out_ref[pl.ds(back_rows(t, j), SLAB, stride=BACK), :] = total[
                t * SLAB : (t + 1) * SLAB, j * LANES : (j + 1) * LANES
            ]


def update_kernel(got_ref, out_hbm, cells, packed, gain, local_ref, sems):
    members = out_hbm.shape[0]
    wide = TILES * LANES
    copies = [
        pltpu.make_async_copy(
            local_ref.at[t], out_hbm.at[:, pl.ds(t * wide, wide)], sems.at[t]
        )
        for t in range(2)
    ]
    lane = lane_of(RUN)
    for t in range(2):
        for d, tile, first, rows in pieces(members):
            cells[first : first + rows, tile * LANES : (tile + 1) * LANES] = got_ref[
                d, t * HALF : t * HALF + rows, :
            ]
        for d in range(SLAB):
            near, rest = back_rows(t, 0), back_rows(t, 3)
            packed[d * SHARE : d * SHARE + 3, :] = got_ref[d, near : near + 3, :]
            packed[d * SHARE + 3 : d * SHARE + 5, :] = got_ref[d, rest : rest + 2, :]
        for g in range(SETS):
            halves = [None, None]
            for f in range(GROUPS):
                part = pltpu.roll(packed[f * RUN : (f + 1) * RUN, :], (f - g) * WIDTH % LANES, 1)
                for h in range(2):
                    start = f * WIDTH - h * LANES
                    if start < LANES and start + WIDTH > 0:
                        halves[h] = (
                            part if halves[h] is None else jnp.where(lane >= start, part, halves[h])
                        )
            for h in range(2):
                gain[g * RUN : (g + 1) * RUN, h * LANES : (h + 1) * LANES] = halves[h]
        values = cells[...]
        anomaly = values - jnp.mean(values, axis=0, keepdims=True)
        local = lax.dot_general(
            gain[...],
            anomaly,
            (((0,), (0,)), ((), ())),
            precision=HIGHEST,
            preferred_element_type=jnp.float32,
        )
        local_ref[t] = local[0:members, :] * jnp.float32(1.0 / (members - 1.0))
        copies[t].start()
    for copy in copies:
        copy.wait()


VMEM = pl.BlockSpec(memory_space=pltpu.VMEM)
HBM = pl.BlockSpec(memory_space=pltpu.HBM)
SMEM = pl.BlockSpec(memory_space=pltpu.SMEM)


def call(kernel, shapes, in_specs, scratch=(), aliases=None, out_spec=VMEM, limit=40):
    many = isinstance(shapes, list)
    outs = [jax.ShapeDtypeStruct(shape, jnp.float32) for shape in (shapes if many else [shapes])]
    return pl.pallas_call(
        kernel,
        out_shape=outs if many else outs[0],
        in_specs=in_specs,
        out_specs=[out_spec] * len(outs) if many else out_spec,
        scratch_shapes=list(scratch),
        input_output_aliases=aliases or {},
        compiler_params=pltpu.CompilerParams(vmem_limit_bytes=limit * 1024 * 1024),
    )


def scratch(rows, columns, dtype=jnp.float32):
    return pltpu.VMEM((rows, columns), dtype)


def per_device(ensemble, predicted, innovation, taper_level, slot_order):
    members = ensemble.shape[0]
    blocks = slot_order.shape[1]
    data_blocks = taper_level.shape[0]
    slabs = data_blocks // SLAB
    regions = 2 * SLAB
    groups = [[s * SLAB + a for a in range(SLAB)] for s in range(slabs)]
    slab = lax.axis_index(BOTH) // SLAB

    def shift(x, by):
        pairs = [
            (s * SLAB + a, (s + by) % slabs * SLAB + a) for s in range(slabs) for a in range(SLAB)
        ]
        return lax.ppermute(x, BOTH, pairs)

    def exchange(x):
        return lax.all_to_all(
            x, BOTH, split_axis=0, concat_axis=0, tiled=True, axis_index_groups=groups
        )

    columns = lax.dynamic_slice_in_dim(taper_level, slab * regions, regions, 1)
    level = jnp.concatenate(
        [
            lax.dynamic_slice_in_dim(columns, (slab + by) % slabs * SLAB, SLAB, 0)
            for by in (0, -1, 1, 2)
        ],
        axis=0,
    ).T

    sent = call(
        pack_kernel,
        (SLAB, SENT, LANES),
        [HBM] * 4,
        [
            scratch(members, 2 * LANES),
            scratch(GROUPS * RUN, LANES),
            scratch(1, LANES),
            scratch(*predicted.shape, predicted.dtype),
            scratch(*innovation.shape, innovation.dtype),
            scratch(*ensemble.shape),
            scratch(*slot_order.shape, slot_order.dtype),
            pltpu.SemaphoreType.DMA((3, CUTS)),
        ],
        limit=62,
    )(predicted, innovation, ensemble, slot_order)
    got = exchange(sent)
    flat = got.reshape(SLAB * SENT, LANES)
    slots = got[:: SLAB // 4, SENT - 1, 0:blocks].astype(jnp.int32)

    x0 = call(turn_kernel, (SLAB, SHARE * LANES), [VMEM])(flat)
    half = SLAB // 2
    low, high = x0[:half], x0[half:]
    x1a = shift(low, 1)
    x2b = shift(high, -1)
    x1b = shift(high, 1)
    x2a = shift(low, -1)
    x3 = shift(x1a, 1)
    x4 = shift(x2b, -1)
    taper, back = call(
        sort_kernel,
        [(regions, data_blocks), (SLAB * BACK, LANES)],
        [SMEM, VMEM, VMEM],
        [scratch(regions, data_blocks, jnp.int32)],
    )(slots, level, flat)
    near = call(near_kernel, (regions, SHARE * LANES), [VMEM] * 6)(taper, x0, x1a, x1b, x2a, x2b)
    back = call(far_kernel, (SLAB * BACK, LANES), [VMEM] * 5, aliases={4: 0})(
        taper, near, x3, x4, back
    )
    arrived = exchange(back.reshape(SLAB, BACK, LANES))
    return call(
        update_kernel,
        ensemble.shape,
        [VMEM],
        [
            scratch(members, TILES * LANES),
            scratch(GROUPS * RUN, LANES),
            scratch(members, 2 * LANES),
            pltpu.VMEM((2, members, TILES * LANES), jnp.float32),
            pltpu.SemaphoreType.DMA((2,)),
        ],
        out_spec=HBM,
    )(arrived)


def solution(mesh):
    return jax.shard_map(
        per_device,
        mesh=mesh,
        in_specs=(
            P(None, BOTH),
            P(None, BOTH),
            P(None, BOTH),
            P(),
            P("dp", None),
        ),
        out_specs=P(None, BOTH),
        check_vma=False,
    )
```

```python
import functools

import jax
import jax.numpy as jnp
from jax import lax
from jax.experimental import pallas as pl
from jax.experimental.pallas import tpu as pltpu
from jax.sharding import PartitionSpec as P

LEVELS = 4
LANES = 128
HIGHEST = lax.Precision.HIGHEST
BOTH = ("dp", "region")


def taper_table(levels):
    values = []
    for level in range(levels + 1):
        z = 2.0 * (levels - level) / levels
        if z <= 1.0:
            value = -(z**5) / 4.0 + z**4 / 2.0 + 5.0 * z**3 / 8.0 - 5.0 * z**2 / 3.0 + 1.0
        else:
            value = (
                z**5 / 12.0
                - z**4 / 2.0
                + 5.0 * z**3 / 8.0
                + 5.0 * z**2 / 3.0
                - 5.0 * z
                + 4.0
                - 2.0 / (3.0 * z)
            )
        values.append(max(value, 0.0))
    return values


TABLE = taper_table(LEVELS)

SLAB = 64
CHIPS = 32
SHARE = 10
PIECE = 25
HALF = 32
SENT = 2 * HALF
BACK = 72
TILES = 4
WIDTH = 25
SETS = 5
GROUPS = 8
RUN = 40


def lane_of(rows):
    return lax.broadcasted_iota(jnp.int32, (rows, LANES), 1)


def sent_row(j):
    return j // 5 * HALF + PIECE + j % 5


SLOT_ROW = SENT - 2
NEAR = HALF - PIECE


def back_row(t, j):
    return t * HALF + PIECE + j if j < NEAR else SENT + t * (SHARE - NEAR) + j - NEAR


def pieces():
    count = CHIPS // TILES
    for q in range(CHIPS):
        yield q, q // count, q % count * PIECE


def slab_index():
    return lax.div(lax.axis_index("dp"), SLAB // lax.axis_size("region"))


def pack_kernel(
    y_hbm,
    w_hbm,
    ens_hbm,
    slot_hbm,
    level_hbm,
    out_ref,
    level_ref,
    gain,
    packed,
    order,
    y_ref,
    w_ref,
    ens_ref,
    slot_ref,
    sems,
):
    members = ens_ref.shape[0]
    slabs = level_ref.shape[0] // SLAB
    slab = slab_index()
    regions = pl.ds(pl.multiple_of(slab * (2 * SLAB), 2 * SLAB), 2 * SLAB)
    early = [
        pltpu.make_async_copy(ens_hbm, ens_ref, sems.at[0]),
        pltpu.make_async_copy(slot_hbm, slot_ref, sems.at[1]),
    ]
    late = [
        pltpu.make_async_copy(y_hbm, y_ref, sems.at[2]),
        pltpu.make_async_copy(w_hbm, w_ref, sems.at[3]),
    ]
    for i, by in enumerate((0, slabs - 1, 1, 2)):
        first = pl.multiple_of(lax.rem(slab + by, slabs) * SLAB, SLAB)
        late.append(
            pltpu.make_async_copy(
                level_hbm.at[pl.ds(first, SLAB), regions],
                level_ref.at[pl.ds(i * SLAB, SLAB)],
                sems.at[4 + i],
            )
        )
    for copy in early + late:
        copy.start()
    for copy in early:
        copy.wait()
    for q, tile, first in pieces():
        for k in range(2):
            column = (k * TILES + tile) * LANES
            out_ref[q, k * HALF : k * HALF + PIECE, :] = ens_ref[
                first : first + PIECE, column : column + LANES
            ]
    for copy in late:
        copy.wait()
    gain[:, 0:members] = lax.dot_general(
        w_ref[...], y_ref[...], (((1,), (1,)), ((), ())), preferred_element_type=jnp.float32
    )
    order[:, 0 : slot_ref.shape[1]] = slot_ref[...].astype(jnp.float32)
    lane = lane_of(RUN)
    for f in range(GROUPS):
        total = None
        for g in range(SETS):
            low = gain[g * RUN : (g + 1) * RUN, 0:LANES]
            high = gain[g * RUN : (g + 1) * RUN, LANES : 2 * LANES]
            start, end = f * WIDTH, (f + 1) * WIDTH
            if end <= LANES:
                part = low
            elif start >= LANES:
                part = high
            else:
                part = jnp.where(lane >= start, low, high)
            part = pltpu.roll(part, (g - f) * WIDTH % LANES, 1)
            total = part if total is None else jnp.where(lane >= g * WIDTH, part, total)
        packed[f * RUN : (f + 1) * RUN, :] = total
    for q in range(CHIPS):
        for j in range(0, SHARE, 5):
            out_ref[q, sent_row(j) : sent_row(j) + 5, :] = packed[
                q * SHARE + j : q * SHARE + j + 5, :
            ]
        out_ref[q, SLOT_ROW : SLOT_ROW + 1, :] = order[...]


def turn_kernel(got_ref, out_ref):
    for j in range(SHARE):
        out_ref[:, j * LANES : (j + 1) * LANES] = got_ref[
            pl.ds(sent_row(j), CHIPS, stride=SENT), :
        ]


def core_index():
    return lax.rem(lax.axis_index("region"), 2)


def sort_kernel(
    slot_ref, level_ref, own_ref, other_ref, taper_ref, out_ref, weight, row, ordered, blocks
):
    slabs = slot_ref.shape[0]
    core = core_index()
    levels = level_ref[...]
    total = jnp.zeros(levels.shape, jnp.float32)
    for value in range(LEVELS + 1):
        total = jnp.where(levels == value, jnp.float32(TABLE[value]), total)
    weight[...] = total
    count = levels.shape[0] // 2
    even = weight[pl.ds(0, count, stride=2), :]
    odd = weight[pl.ds(1, count, stride=2), :]
    row[...] = jnp.where(core == 0, even, odd).T
    per = CHIPS // slabs
    for got_ref, side in ((own_ref, core), (other_ref, 1 - core)):
        for k in range(CHIPS):
            for h in range(2):
                region = k % per * 4 + h + 2 * side
                dest = slot_ref[k // per, region] + k // per * 4 * per
                t = lax.bitwise_and(dest, 1)
                away = lax.bitwise_xor(lax.bitwise_and(lax.shift_right_logical(dest, 1), 1), core)
                place = away * SLAB + t * CHIPS + lax.shift_right_logical(dest, 2)
                ordered[pl.ds(place, 1), :] = row[pl.ds(region + k // per * 4 * per, 1), :]
                first = pl.multiple_of(place * HALF, HALF)
                blocks[pl.ds(first, HALF), :] = got_ref[
                    (2 * k + h) * HALF : (2 * k + h + 1) * HALF, :
                ]
    taper_ref[...] = ordered[...]
    for t in range(2):
        for p in range(CHIPS):
            out_ref[p * BACK + t * HALF : p * BACK + (t + 1) * HALF, :] = blocks[
                (t * CHIPS + p) * HALF : (t * CHIPS + p + 1) * HALF, :
            ]


def weigh(taper, x):
    return lax.dot_general(
        taper,
        x,
        (((1,), (0,)), ((), ())),
        precision=HIGHEST,
        preferred_element_type=jnp.float32,
    )


def near_kernel(taper_ref, x0_ref, x1a_ref, x1b_ref, x2a_ref, x2b_ref, out_ref):
    refs = (x0_ref, x1a_ref, x1b_ref, x2a_ref, x2b_ref)
    x = jnp.concatenate([ref[...] for ref in refs], axis=0)
    out_ref[...] = weigh(taper_ref[:, 0 : 3 * CHIPS], x)


def far_kernel(rows, taper_ref, near_ref, x3_ref, x4_ref, out_ref):
    far = jnp.concatenate([x3_ref[...], x4_ref[...]], axis=0)
    out_ref[...] = near_ref[rows, :] + weigh(taper_ref[rows, 3 * CHIPS : 4 * CHIPS], far)


def place_kernel(keep_ref, taken_ref, back_ref, out_ref):
    del back_ref
    for t in range(2):
        rows = slice(t * CHIPS, (t + 1) * CHIPS)
        for j in range(SHARE):
            columns = slice(j * LANES, (j + 1) * LANES)
            out_ref[pl.ds(back_row(t, j), CHIPS, stride=BACK), :] = (
                keep_ref[rows, columns] + taken_ref[rows, columns]
            )


def update_kernel(got_ref, out_hbm, cells, packed, gain, local_ref, sems):
    members = out_hbm.shape[0]
    wide = TILES * LANES
    copies = [
        pltpu.make_async_copy(
            local_ref.at[t], out_hbm.at[:, pl.ds(t * wide, wide)], sems.at[t]
        )
        for t in range(2)
    ]
    lane = lane_of(RUN)
    for t in range(2):
        for q, tile, first in pieces():
            cells[first : first + PIECE, tile * LANES : (tile + 1) * LANES] = got_ref[
                q, t * HALF : t * HALF + PIECE, :
            ]
            for start, end in ((0, NEAR), (NEAR, SHARE)):
                at = back_row(t, start)
                packed[q * SHARE + start : q * SHARE + end, :] = got_ref[
                    q, at : at + end - start, :
                ]
        for g in range(SETS):
            halves = [None, None]
            for f in range(GROUPS):
                part = pltpu.roll(packed[f * RUN : (f + 1) * RUN, :], (f - g) * WIDTH % LANES, 1)
                for h in range(2):
                    start = f * WIDTH - h * LANES
                    if start < LANES and start + WIDTH > 0:
                        halves[h] = (
                            part if halves[h] is None else jnp.where(lane >= start, part, halves[h])
                        )
            for h in range(2):
                gain[g * RUN : (g + 1) * RUN, h * LANES : (h + 1) * LANES] = halves[h]
        values = cells[...]
        anomaly = values - jnp.mean(values, axis=0, keepdims=True)
        local = lax.dot_general(
            gain[:, 0:members],
            anomaly,
            (((1,), (0,)), ((), ())),
            precision=HIGHEST,
            preferred_element_type=jnp.float32,
        )
        local_ref[t] = local * jnp.float32(1.0 / (members - 1.0))
        copies[t].start()
    for copy in copies:
        copy.wait()


VMEM = pl.BlockSpec(memory_space=pltpu.VMEM)
HBM = pl.BlockSpec(memory_space=pltpu.HBM)
SMEM = pl.BlockSpec(memory_space=pltpu.SMEM)


def call(kernel, shapes, in_specs, scratch=(), aliases=None, out_spec=VMEM, vmem_out=False):
    many = isinstance(shapes, list)
    outs = []
    for shape in shapes if many else [shapes]:
        dims, dtype = shape if isinstance(shape[0], tuple) else (shape, jnp.float32)
        outs.append((pltpu.VMEM if vmem_out else jax.ShapeDtypeStruct)(dims, dtype))
    return pl.pallas_call(
        kernel,
        out_shape=outs if many else outs[0],
        in_specs=in_specs,
        out_specs=[out_spec] * len(outs) if many else out_spec,
        scratch_shapes=list(scratch),
        input_output_aliases=aliases or {},
        compiler_params=pltpu.CompilerParams(vmem_limit_bytes=40 * 1024 * 1024),
    )


def scratch(rows, columns, dtype=jnp.float32):
    return pltpu.VMEM((rows, columns), dtype)


def per_device(ensemble, predicted, innovation, taper_level, slot_order):
    members = ensemble.shape[0]
    blocks = slot_order.shape[1]
    data_blocks = taper_level.shape[0]
    slabs = data_blocks // SLAB
    regions = 2 * SLAB
    groups = [[s * SLAB + 2 * k + c for k in range(CHIPS)] for s in range(slabs) for c in range(2)]

    def shift(x, by):
        pairs = [
            (s * SLAB + a, (s + by) % slabs * SLAB + a) for s in range(slabs) for a in range(SLAB)
        ]
        return lax.ppermute(x, BOTH, pairs)

    def swap(x):
        return lax.ppermute(x, BOTH, [(i, i ^ 1) for i in range(data_blocks)])

    def exchange(x):
        return lax.all_to_all(
            x, BOTH, split_axis=0, concat_axis=0, tiled=True, axis_index_groups=groups
        )

    sent, level = call(
        pack_kernel,
        [(CHIPS, SENT, LANES), ((data_blocks, regions), jnp.int32)],
        [HBM] * 5,
        [
            scratch(members, 2 * LANES),
            scratch(GROUPS * RUN, LANES),
            scratch(1, LANES),
            scratch(*predicted.shape, predicted.dtype),
            scratch(*innovation.shape, innovation.dtype),
            scratch(*ensemble.shape),
            scratch(*slot_order.shape, slot_order.dtype),
            pltpu.SemaphoreType.DMA((4 + slabs,)),
        ],
        vmem_out=True,
    )(
        *(
            pltpu.with_memory_space_constraint(x, pltpu.HBM)
            for x in (predicted, innovation, ensemble, slot_order, taper_level)
        )
    )
    got = exchange(sent)
    own = got.reshape(CHIPS * SENT, LANES)
    slots = got[:: CHIPS // slabs, SLOT_ROW, 0:blocks].astype(jnp.int32)

    part = SHARE * LANES
    x0 = call(turn_kernel, (CHIPS, part), [VMEM])(own)
    low, high = x0[: CHIPS // 2], x0[CHIPS // 2 :]
    x1a = shift(low, 1)
    x2b = shift(high, -1)
    x1b = shift(high, 1)
    x2a = shift(low, -1)
    x3 = shift(x1a, 1)
    x4 = shift(x2b, -1)
    other = swap(own)
    taper, back = call(
        sort_kernel,
        [(regions, data_blocks // 2), (CHIPS * BACK, LANES)],
        [SMEM, VMEM, VMEM, VMEM],
        [
            scratch(data_blocks, regions),
            scratch(regions, data_blocks // 2),
            scratch(regions, data_blocks // 2),
            scratch(regions * HALF, LANES),
        ],
    )(slots, level, own, other)
    near = call(near_kernel, (regions, part), [VMEM] * 6)(taper, x0, x1a, x1b, x2a, x2b)
    keep, give = (
        call(functools.partial(far_kernel, rows), (SLAB, part), [VMEM] * 4)(taper, near, x3, x4)
        for rows in (slice(0, SLAB), slice(SLAB, 2 * SLAB))
    )
    back = call(place_kernel, (CHIPS * BACK, LANES), [VMEM] * 3, aliases={2: 0})(
        keep, swap(give), back
    )
    arrived = exchange(back.reshape(CHIPS, BACK, LANES))
    return call(
        update_kernel,
        ensemble.shape,
        [VMEM],
        [
            scratch(members, TILES * LANES),
            scratch(GROUPS * RUN, LANES),
            scratch(members, 2 * LANES),
            pltpu.VMEM((2, members, TILES * LANES), jnp.float32),
            pltpu.SemaphoreType.DMA((2,)),
        ],
        out_spec=HBM,
    )(arrived)


def solution(mesh):
    return jax.shard_map(
        per_device,
        mesh=mesh,
        in_specs=(
            P(None, BOTH),
            P(None, BOTH),
            P(None, BOTH),
            P(),
            P("dp", None),
        ),
        out_specs=P(None, BOTH),
        check_vma=False,
    )
```

```python
import functools

import jax
import jax.numpy as jnp
from jax import lax
from jax.experimental import pallas as pl
from jax.experimental.pallas import tpu as pltpu
from jax.sharding import PartitionSpec as P

LEVELS = 4
LANES = 128
HIGHEST = lax.Precision.HIGHEST
BOTH = ("dp", "region")


def taper_table(levels):
    values = []
    for level in range(levels + 1):
        z = 2.0 * (levels - level) / levels
        if z <= 1.0:
            value = -(z**5) / 4.0 + z**4 / 2.0 + 5.0 * z**3 / 8.0 - 5.0 * z**2 / 3.0 + 1.0
        else:
            value = (
                z**5 / 12.0
                - z**4 / 2.0
                + 5.0 * z**3 / 8.0
                + 5.0 * z**2 / 3.0
                - 5.0 * z
                + 4.0
                - 2.0 / (3.0 * z)
            )
        values.append(max(value, 0.0))
    return values


TABLE = taper_table(LEVELS)

SLAB = 64
CHIPS = 32
SHARE = 10
PIECE = 25
HALF = 32
SENT = 2 * HALF
BACK = 72
TILES = 4
WIDTH = 25
SETS = 5
GROUPS = 8
RUN = 40


def lane_of(rows):
    return lax.broadcasted_iota(jnp.int32, (rows, LANES), 1)


def sent_row(j):
    return j // 5 * HALF + PIECE + j % 5


SLOT_ROW = SENT - 2
NEAR = HALF - PIECE


def back_row(t, j):
    return t * HALF + PIECE + j if j < NEAR else SENT + t * (SHARE - NEAR) + j - NEAR


def pieces():
    count = CHIPS // TILES
    for q in range(CHIPS):
        yield q, q // count, q % count * PIECE


def core_index():
    return lax.rem(lax.axis_index("region"), 2)


def slab_index():
    return lax.div(lax.axis_index("dp"), SLAB // lax.axis_size("region"))


def pack_kernel(
    y_hbm,
    w_hbm,
    ens_hbm,
    slot_hbm,
    level_hbm,
    out_ref,
    level_ref,
    gain,
    packed,
    order,
    y_ref,
    w_ref,
    ens_ref,
    slot_ref,
    sems,
):
    members = ens_ref.shape[0]
    slabs = level_ref.shape[0] // SLAB
    slab = slab_index()
    regions = pl.ds(pl.multiple_of(slab * (2 * SLAB), 2 * SLAB), 2 * SLAB)
    early = [
        pltpu.make_async_copy(ens_hbm, ens_ref, sems.at[0]),
        pltpu.make_async_copy(slot_hbm, slot_ref, sems.at[1]),
    ]
    late = [
        pltpu.make_async_copy(y_hbm, y_ref, sems.at[2]),
        pltpu.make_async_copy(w_hbm, w_ref, sems.at[3]),
    ]
    core = core_index()
    ahead = 1 - 2 * core
    half = SLAB // 2
    for i, by in enumerate((0, slabs - ahead, slabs + ahead, 2)):
        first = lax.rem(slab + by, slabs) * SLAB
        for h in range(2):
            row = pl.multiple_of(first + lax.rem(core + h, 2) * half, half)
            late.append(
                pltpu.make_async_copy(
                    level_hbm.at[pl.ds(row, half), regions],
                    level_ref.at[pl.ds(i * SLAB + h * half, half)],
                    sems.at[4 + 2 * i + h],
                )
            )
    for copy in early + late:
        copy.start()
    for copy in early:
        copy.wait()
    for q, tile, first in pieces():
        for k in range(2):
            column = (k * TILES + tile) * LANES
            out_ref[q, k * HALF : k * HALF + PIECE, :] = ens_ref[
                first : first + PIECE, column : column + LANES
            ]
    for copy in late:
        copy.wait()
    gain[:, 0:members] = lax.dot_general(
        w_ref[...], y_ref[...], (((1,), (1,)), ((), ())), preferred_element_type=jnp.float32
    )
    order[:, 0 : slot_ref.shape[1]] = slot_ref[...].astype(jnp.float32)
    lane = lane_of(RUN)
    for f in range(GROUPS):
        total = None
        for g in range(SETS):
            low = gain[g * RUN : (g + 1) * RUN, 0:LANES]
            high = gain[g * RUN : (g + 1) * RUN, LANES : 2 * LANES]
            start, end = f * WIDTH, (f + 1) * WIDTH
            if end <= LANES:
                part = low
            elif start >= LANES:
                part = high
            else:
                part = jnp.where(lane >= start, low, high)
            part = pltpu.roll(part, (g - f) * WIDTH % LANES, 1)
            total = part if total is None else jnp.where(lane >= g * WIDTH, part, total)
        packed[f * RUN : (f + 1) * RUN, :] = total
    for q in range(CHIPS):
        for j in range(0, SHARE, 5):
            out_ref[q, sent_row(j) : sent_row(j) + 5, :] = packed[
                q * SHARE + j : q * SHARE + j + 5, :
            ]
        out_ref[q, SLOT_ROW : SLOT_ROW + 1, :] = order[...]


def turn_kernel(got_ref, first_ref, second_ref):
    core = core_index()
    half = CHIPS // 2
    for j in range(SHARE):
        low = got_ref[pl.ds(sent_row(j), half, stride=SENT), :]
        high = got_ref[pl.ds(half * SENT + sent_row(j), half, stride=SENT), :]
        columns = slice(j * LANES, (j + 1) * LANES)
        first_ref[:, columns] = jnp.where(core == 0, low, high)
        second_ref[:, columns] = jnp.where(core == 0, high, low)


def sort_kernel(
    slot_ref, level_ref, own_ref, other_ref, taper_ref, out_ref, weight, row, ordered, blocks
):
    slabs = slot_ref.shape[0]
    core = core_index()
    levels = level_ref[...]
    total = jnp.zeros(levels.shape, jnp.float32)
    for value in range(LEVELS + 1):
        total = jnp.where(levels == value, jnp.float32(TABLE[value]), total)
    weight[...] = total
    count = levels.shape[0] // 2
    even = weight[pl.ds(0, count, stride=2), :]
    odd = weight[pl.ds(1, count, stride=2), :]
    row[...] = jnp.where(core == 0, even, odd).T
    per = CHIPS // slabs
    for got_ref, side in ((own_ref, core), (other_ref, 1 - core)):
        for k in range(CHIPS):
            for h in range(2):
                region = k % per * 4 + h + 2 * side
                dest = slot_ref[k // per, region] + k // per * 4 * per
                t = lax.bitwise_and(dest, 1)
                away = lax.bitwise_xor(lax.bitwise_and(lax.shift_right_logical(dest, 1), 1), core)
                place = away * SLAB + t * CHIPS + lax.shift_right_logical(dest, 2)
                ordered[pl.ds(place, 1), :] = row[pl.ds(region + k // per * 4 * per, 1), :]
                first = pl.multiple_of(place * HALF, HALF)
                blocks[pl.ds(first, HALF), :] = got_ref[
                    (2 * k + h) * HALF : (2 * k + h + 1) * HALF, :
                ]
    taper_ref[...] = ordered[...]
    for t in range(2):
        for p in range(CHIPS):
            out_ref[p * BACK + t * HALF : p * BACK + (t + 1) * HALF, :] = blocks[
                (t * CHIPS + p) * HALF : (t * CHIPS + p + 1) * HALF, :
            ]


def weigh(taper, x):
    return lax.dot_general(
        taper,
        x,
        (((1,), (0,)), ((), ())),
        precision=HIGHEST,
        preferred_element_type=jnp.float32,
    )


def near_kernel(taper_ref, *refs):
    x = jnp.concatenate([ref[...] for ref in refs[:-1]], axis=0)
    refs[-1][...] = weigh(taper_ref[:, 0 : 3 * CHIPS], x)


def far_kernel(rows, taper_ref, near_ref, x3_ref, x4_ref, out_ref):
    far = jnp.concatenate([x3_ref[...], x4_ref[...]], axis=0)
    out_ref[...] = near_ref[rows, :] + weigh(taper_ref[rows, 3 * CHIPS : 4 * CHIPS], far)


def place_kernel(keep_ref, taken_ref, back_ref, out_ref):
    del back_ref
    for t in range(2):
        rows = slice(t * CHIPS, (t + 1) * CHIPS)
        for j in range(SHARE):
            columns = slice(j * LANES, (j + 1) * LANES)
            out_ref[pl.ds(back_row(t, j), CHIPS, stride=BACK), :] = (
                keep_ref[rows, columns] + taken_ref[rows, columns]
            )


def update_kernel(got_ref, out_hbm, cells, packed, gain, local_ref, sems):
    members = out_hbm.shape[0]
    wide = TILES * LANES
    copies = [
        pltpu.make_async_copy(
            local_ref.at[t], out_hbm.at[:, pl.ds(t * wide, wide)], sems.at[t]
        )
        for t in range(2)
    ]
    lane = lane_of(RUN)
    for t in range(2):
        for q, tile, first in pieces():
            cells[first : first + PIECE, tile * LANES : (tile + 1) * LANES] = got_ref[
                q, t * HALF : t * HALF + PIECE, :
            ]
            for start, end in ((0, NEAR), (NEAR, SHARE)):
                at = back_row(t, start)
                packed[q * SHARE + start : q * SHARE + end, :] = got_ref[
                    q, at : at + end - start, :
                ]
        for g in range(SETS):
            halves = [None, None]
            for f in range(GROUPS):
                part = pltpu.roll(packed[f * RUN : (f + 1) * RUN, :], (f - g) * WIDTH % LANES, 1)
                for h in range(2):
                    start = f * WIDTH - h * LANES
                    if start < LANES and start + WIDTH > 0:
                        halves[h] = (
                            part if halves[h] is None else jnp.where(lane >= start, part, halves[h])
                        )
            halves[1] = jnp.where(lane < members - LANES, halves[1], 0.0)
            for h in range(2):
                gain[g * RUN : (g + 1) * RUN, h * LANES : (h + 1) * LANES] = halves[h]
        values = cells[...]
        anomaly = values - jnp.mean(values, axis=0, keepdims=True)
        local = lax.dot_general(
            gain[:, 0:members],
            anomaly,
            (((1,), (0,)), ((), ())),
            precision=HIGHEST,
            preferred_element_type=jnp.float32,
        )
        local_ref[t] = local * jnp.float32(1.0 / (members - 1.0))
        copies[t].start()
    for copy in copies:
        copy.wait()


VMEM = pl.BlockSpec(memory_space=pltpu.VMEM)
HBM = pl.BlockSpec(memory_space=pltpu.HBM)
SMEM = pl.BlockSpec(memory_space=pltpu.SMEM)


def call(kernel, shapes, in_specs, scratch=(), aliases=None, out_spec=VMEM, vmem_out=False):
    many = isinstance(shapes, list)
    outs = []
    for shape in shapes if many else [shapes]:
        dims, dtype = shape if isinstance(shape[0], tuple) else (shape, jnp.float32)
        outs.append((pltpu.VMEM if vmem_out else jax.ShapeDtypeStruct)(dims, dtype))
    return pl.pallas_call(
        kernel,
        out_shape=outs if many else outs[0],
        in_specs=in_specs,
        out_specs=[out_spec] * len(outs) if many else out_spec,
        scratch_shapes=list(scratch),
        input_output_aliases=aliases or {},
        compiler_params=pltpu.CompilerParams(vmem_limit_bytes=40 * 1024 * 1024),
    )


def scratch(rows, columns, dtype=jnp.float32):
    return pltpu.VMEM((rows, columns), dtype)


def per_device(ensemble, predicted, innovation, taper_level, slot_order):
    members = ensemble.shape[0]
    blocks = slot_order.shape[1]
    data_blocks = taper_level.shape[0]
    slabs = data_blocks // SLAB
    regions = 2 * SLAB
    groups = [[s * SLAB + 2 * k + c for k in range(CHIPS)] for s in range(slabs) for c in range(2)]

    def shift(x, by):
        pairs = [
            (s * SLAB + a, (s + by * (1 - 2 * (a % 2))) % slabs * SLAB + a)
            for s in range(slabs)
            for a in range(SLAB)
        ]
        return lax.ppermute(x, BOTH, pairs)

    def swap(x):
        return lax.ppermute(x, BOTH, [(i, i ^ 1) for i in range(data_blocks)])

    def exchange(x):
        return lax.all_to_all(
            x, BOTH, split_axis=0, concat_axis=0, tiled=True, axis_index_groups=groups
        )

    sent, level = call(
        pack_kernel,
        [(CHIPS, SENT, LANES), ((data_blocks, regions), jnp.int32)],
        [HBM] * 5,
        [
            scratch(members, 2 * LANES),
            scratch(GROUPS * RUN, LANES),
            scratch(1, LANES),
            scratch(*predicted.shape, predicted.dtype),
            scratch(*innovation.shape, innovation.dtype),
            scratch(*ensemble.shape),
            scratch(*slot_order.shape, slot_order.dtype),
            pltpu.SemaphoreType.DMA((4 + 2 * slabs,)),
        ],
        vmem_out=True,
    )(
        *(
            pltpu.with_memory_space_constraint(x, pltpu.HBM)
            for x in (predicted, innovation, ensemble, slot_order, taper_level)
        )
    )
    got = exchange(sent)
    own = got.reshape(CHIPS * SENT, LANES)
    slots = got[:: CHIPS // slabs, SLOT_ROW, 0:blocks].astype(jnp.int32)

    part = SHARE * LANES
    first, second = call(turn_kernel, [(CHIPS // 2, part)] * 2, [VMEM])(own)
    x1a = shift(first, 1)
    x1b = shift(second, 1)
    x2b = shift(second, -1)
    x2a = shift(first, -1)
    x3 = shift(x1a, 1)
    x4 = shift(x2b, -1)
    other = swap(own)
    taper, back = call(
        sort_kernel,
        [(regions, data_blocks // 2), (CHIPS * BACK, LANES)],
        [SMEM, VMEM, VMEM, VMEM],
        [
            scratch(data_blocks, regions),
            scratch(regions, data_blocks // 2),
            scratch(regions, data_blocks // 2),
            scratch(regions * HALF, LANES),
        ],
    )(slots, level, own, other)
    near = call(near_kernel, (regions, part), [VMEM] * 7)(
        taper, first, second, x1a, x1b, x2a, x2b
    )
    keep, give = (
        call(functools.partial(far_kernel, rows), (SLAB, part), [VMEM] * 4)(taper, near, x3, x4)
        for rows in (slice(0, SLAB), slice(SLAB, 2 * SLAB))
    )
    back = call(place_kernel, (CHIPS * BACK, LANES), [VMEM] * 3, aliases={2: 0})(
        keep, swap(give), back
    )
    arrived = exchange(back.reshape(CHIPS, BACK, LANES))
    return call(
        update_kernel,
        ensemble.shape,
        [VMEM],
        [
            scratch(members, TILES * LANES),
            scratch(GROUPS * RUN, LANES),
            scratch(members, 2 * LANES),
            pltpu.VMEM((2, members, TILES * LANES), jnp.float32),
            pltpu.SemaphoreType.DMA((2,)),
        ],
        out_spec=HBM,
    )(arrived)


def solution(mesh):
    return jax.shard_map(
        per_device,
        mesh=mesh,
        in_specs=(
            P(None, BOTH),
            P(None, BOTH),
            P(None, BOTH),
            P(),
            P("dp", None),
        ),
        out_specs=P(None, BOTH),
        check_vma=False,
    )
```

```python
import functools

import jax
import jax.numpy as jnp
from jax import lax
from jax.experimental import pallas as pl
from jax.experimental.pallas import tpu as pltpu
from jax.sharding import PartitionSpec as P

LEVELS = 4
LANES = 128
HIGHEST = lax.Precision.HIGHEST
BOTH = ("dp", "region")


def taper_table(levels):
    values = []
    for level in range(levels + 1):
        z = 2.0 * (levels - level) / levels
        if z <= 1.0:
            value = -(z**5) / 4.0 + z**4 / 2.0 + 5.0 * z**3 / 8.0 - 5.0 * z**2 / 3.0 + 1.0
        else:
            value = (
                z**5 / 12.0
                - z**4 / 2.0
                + 5.0 * z**3 / 8.0
                + 5.0 * z**2 / 3.0
                - 5.0 * z
                + 4.0
                - 2.0 / (3.0 * z)
            )
        values.append(max(value, 0.0))
    return values


TABLE = taper_table(LEVELS)

SLAB = 64
CHIPS = 32
SHARE = 10
PIECE = 25
HALF = 32
SENT = 2 * HALF
BACK = 72
TILES = 4
WIDTH = 25
SETS = 5
GROUPS = 8
RUN = 40


def lane_of(rows):
    return lax.broadcasted_iota(jnp.int32, (rows, LANES), 1)


def sent_row(j):
    return j // 5 * HALF + PIECE + j % 5


SLOT_ROW = SENT - 2
NEAR = HALF - PIECE


def back_row(t, j):
    return t * HALF + PIECE + j if j < NEAR else SENT + t * (SHARE - NEAR) + j - NEAR


def pieces():
    count = CHIPS // TILES
    for q in range(CHIPS):
        yield q, q // count, q % count * PIECE


def core_index():
    return lax.rem(lax.axis_index("region"), 2)


def slab_index():
    return lax.div(lax.axis_index("dp"), SLAB // lax.axis_size("region"))


def pack_kernel(
    y_hbm,
    w_hbm,
    ens_hbm,
    slot_hbm,
    level_hbm,
    out_ref,
    level_ref,
    gain,
    packed,
    order,
    y_ref,
    w_ref,
    ens_ref,
    slot_ref,
    sems,
):
    members = ens_ref.shape[0]
    slabs = level_ref.shape[0] // SLAB
    slab = slab_index()
    regions = pl.ds(pl.multiple_of(slab * (2 * SLAB), 2 * SLAB), 2 * SLAB)
    early = [
        pltpu.make_async_copy(ens_hbm, ens_ref, sems.at[0]),
        pltpu.make_async_copy(slot_hbm, slot_ref, sems.at[1]),
    ]
    late = [
        pltpu.make_async_copy(y_hbm, y_ref, sems.at[2]),
        pltpu.make_async_copy(w_hbm, w_ref, sems.at[3]),
    ]
    core = core_index()
    ahead = 1 - 2 * core
    half = SLAB // 2
    for i, by in enumerate((0, slabs - ahead, slabs + ahead, 2)):
        first = lax.rem(slab + by, slabs) * SLAB
        for h in range(2):
            row = pl.multiple_of(first + lax.rem(core + h, 2) * half, half)
            late.append(
                pltpu.make_async_copy(
                    level_hbm.at[pl.ds(row, half), regions],
                    level_ref.at[pl.ds(i * SLAB + h * half, half)],
                    sems.at[4 + 2 * i + h],
                )
            )
    for copy in late[:2] + early + late[2:]:
        copy.start()
    for copy in late[:2]:
        copy.wait()
    gain[:, 0:members] = lax.dot_general(
        w_ref[...], y_ref[...], (((1,), (1,)), ((), ())), preferred_element_type=jnp.float32
    )
    lane = lane_of(RUN)
    for f in range(GROUPS):
        total = None
        for g in range(SETS):
            low = gain[g * RUN : (g + 1) * RUN, 0:LANES]
            high = gain[g * RUN : (g + 1) * RUN, LANES : 2 * LANES]
            start, end = f * WIDTH, (f + 1) * WIDTH
            if end <= LANES:
                part = low
            elif start >= LANES:
                part = high
            else:
                part = jnp.where(lane >= start, low, high)
            part = pltpu.roll(part, (g - f) * WIDTH % LANES, 1)
            total = part if total is None else jnp.where(lane >= g * WIDTH, part, total)
        packed[f * RUN : (f + 1) * RUN, :] = total
    for copy in early + late[2:]:
        copy.wait()
    order[:, 0 : slot_ref.shape[1]] = slot_ref[...].astype(jnp.float32)
    for q, tile, first in pieces():
        for k in range(2):
            column = (k * TILES + tile) * LANES
            out_ref[q, k * HALF : k * HALF + PIECE, :] = ens_ref[
                first : first + PIECE, column : column + LANES
            ]
    for q in range(CHIPS):
        for j in range(0, SHARE, 5):
            out_ref[q, sent_row(j) : sent_row(j) + 5, :] = packed[
                q * SHARE + j : q * SHARE + j + 5, :
            ]
        out_ref[q, SLOT_ROW : SLOT_ROW + 1, :] = order[...]


def turn_kernel(got_ref, first_ref, second_ref):
    core = core_index()
    half = CHIPS // 2
    for j in range(SHARE):
        low = got_ref[pl.ds(sent_row(j), half, stride=SENT), :]
        high = got_ref[pl.ds(half * SENT + sent_row(j), half, stride=SENT), :]
        columns = slice(j * LANES, (j + 1) * LANES)
        first_ref[:, columns] = jnp.where(core == 0, low, high)
        second_ref[:, columns] = jnp.where(core == 0, high, low)


def sort_kernel(
    slot_ref, level_ref, own_ref, other_ref, taper_ref, out_ref, weight, row, ordered, blocks
):
    slabs = slot_ref.shape[0]
    core = core_index()
    levels = level_ref[...]
    total = jnp.zeros(levels.shape, jnp.float32)
    for value in range(LEVELS + 1):
        total = jnp.where(levels == value, jnp.float32(TABLE[value]), total)
    weight[...] = total
    count = levels.shape[0] // 2
    even = weight[pl.ds(0, count, stride=2), :]
    odd = weight[pl.ds(1, count, stride=2), :]
    row[...] = jnp.where(core == 0, even, odd).T
    per = CHIPS // slabs
    for got_ref, side in ((own_ref, core), (other_ref, 1 - core)):
        for k in range(CHIPS):
            for h in range(2):
                region = k % per * 4 + h + 2 * side
                dest = slot_ref[k // per, region] + k // per * 4 * per
                t = lax.bitwise_and(dest, 1)
                away = lax.bitwise_xor(lax.bitwise_and(lax.shift_right_logical(dest, 1), 1), core)
                place = away * SLAB + t * CHIPS + lax.shift_right_logical(dest, 2)
                ordered[pl.ds(place, 1), :] = row[pl.ds(region + k // per * 4 * per, 1), :]
                first = pl.multiple_of(place * HALF, HALF)
                blocks[pl.ds(first, HALF), :] = got_ref[
                    (2 * k + h) * HALF : (2 * k + h + 1) * HALF, :
                ]
    taper_ref[...] = ordered[...]
    for t in range(2):
        for p in range(CHIPS):
            out_ref[p * BACK + t * HALF : p * BACK + (t + 1) * HALF, :] = blocks[
                (t * CHIPS + p) * HALF : (t * CHIPS + p + 1) * HALF, :
            ]


def weigh(taper, x):
    return lax.dot_general(
        taper,
        x,
        (((1,), (0,)), ((), ())),
        precision=HIGHEST,
        preferred_element_type=jnp.float32,
    )


def near_kernel(taper_ref, *refs):
    x = jnp.concatenate([ref[...] for ref in refs[:-1]], axis=0)
    refs[-1][...] = weigh(taper_ref[:, 0 : 3 * CHIPS], x)


def far_kernel(rows, taper_ref, near_ref, x3_ref, x4_ref, out_ref):
    far = jnp.concatenate([x3_ref[...], x4_ref[...]], axis=0)
    out_ref[...] = near_ref[rows, :] + weigh(taper_ref[rows, 3 * CHIPS : 4 * CHIPS], far)


def place_kernel(keep_ref, taken_ref, back_ref, out_ref):
    del back_ref
    for t in range(2):
        rows = slice(t * CHIPS, (t + 1) * CHIPS)
        for j in range(SHARE):
            columns = slice(j * LANES, (j + 1) * LANES)
            out_ref[pl.ds(back_row(t, j), CHIPS, stride=BACK), :] = (
                keep_ref[rows, columns] + taken_ref[rows, columns]
            )


def update_kernel(got_ref, out_hbm, cells, packed, gain, local_ref, sems):
    members = out_hbm.shape[0]
    wide = TILES * LANES
    copies = [
        pltpu.make_async_copy(
            local_ref.at[t], out_hbm.at[:, pl.ds(t * wide, wide)], sems.at[t]
        )
        for t in range(2)
    ]
    lane = lane_of(RUN)
    for t in range(2):
        for q, tile, first in pieces():
            cells[first : first + PIECE, tile * LANES : (tile + 1) * LANES] = got_ref[
                q, t * HALF : t * HALF + PIECE, :
            ]
            for start, end in ((0, NEAR), (NEAR, SHARE)):
                at = back_row(t, start)
                packed[q * SHARE + start : q * SHARE + end, :] = got_ref[
                    q, at : at + end - start, :
                ]
        for g in range(SETS):
            halves = [None, None]
            for f in range(GROUPS):
                part = pltpu.roll(packed[f * RUN : (f + 1) * RUN, :], (f - g) * WIDTH % LANES, 1)
                for h in range(2):
                    start = f * WIDTH - h * LANES
                    if start < LANES and start + WIDTH > 0:
                        halves[h] = (
                            part if halves[h] is None else jnp.where(lane >= start, part, halves[h])
                        )
            halves[1] = jnp.where(lane < members - LANES, halves[1], 0.0)
            for h in range(2):
                gain[g * RUN : (g + 1) * RUN, h * LANES : (h + 1) * LANES] = halves[h]
        values = cells[...]
        anomaly = values - jnp.mean(values, axis=0, keepdims=True)
        local = lax.dot_general(
            gain[:, 0:members],
            anomaly,
            (((1,), (0,)), ((), ())),
            precision=HIGHEST,
            preferred_element_type=jnp.float32,
        )
        local_ref[t] = local * jnp.float32(1.0 / (members - 1.0))
        copies[t].start()
    for copy in copies:
        copy.wait()


VMEM = pl.BlockSpec(memory_space=pltpu.VMEM)
HBM = pl.BlockSpec(memory_space=pltpu.HBM)
SMEM = pl.BlockSpec(memory_space=pltpu.SMEM)


def call(kernel, shapes, in_specs, scratch=(), aliases=None, out_spec=VMEM, vmem_out=False):
    many = isinstance(shapes, list)
    outs = []
    for shape in shapes if many else [shapes]:
        dims, dtype = shape if isinstance(shape[0], tuple) else (shape, jnp.float32)
        outs.append((pltpu.VMEM if vmem_out else jax.ShapeDtypeStruct)(dims, dtype))
    return pl.pallas_call(
        kernel,
        out_shape=outs if many else outs[0],
        in_specs=in_specs,
        out_specs=[out_spec] * len(outs) if many else out_spec,
        scratch_shapes=list(scratch),
        input_output_aliases=aliases or {},
        compiler_params=pltpu.CompilerParams(vmem_limit_bytes=40 * 1024 * 1024),
    )


def scratch(rows, columns, dtype=jnp.float32):
    return pltpu.VMEM((rows, columns), dtype)


def per_device(ensemble, predicted, innovation, taper_level, slot_order):
    members = ensemble.shape[0]
    blocks = slot_order.shape[1]
    data_blocks = taper_level.shape[0]
    slabs = data_blocks // SLAB
    regions = 2 * SLAB
    groups = [[s * SLAB + 2 * k + c for k in range(CHIPS)] for s in range(slabs) for c in range(2)]

    def shift(x, by):
        pairs = [
            (s * SLAB + a, (s + by * (1 - 2 * (a % 2))) % slabs * SLAB + a)
            for s in range(slabs)
            for a in range(SLAB)
        ]
        return lax.ppermute(x, BOTH, pairs)

    def swap(x):
        return lax.ppermute(x, BOTH, [(i, i ^ 1) for i in range(data_blocks)])

    def exchange(x):
        return lax.all_to_all(
            x, BOTH, split_axis=0, concat_axis=0, tiled=True, axis_index_groups=groups
        )

    sent, level = call(
        pack_kernel,
        [(CHIPS, SENT, LANES), ((data_blocks, regions), jnp.int32)],
        [HBM] * 5,
        [
            scratch(members, 2 * LANES),
            scratch(GROUPS * RUN, LANES),
            scratch(1, LANES),
            scratch(*predicted.shape, predicted.dtype),
            scratch(*innovation.shape, innovation.dtype),
            scratch(*ensemble.shape),
            scratch(*slot_order.shape, slot_order.dtype),
            pltpu.SemaphoreType.DMA((4 + 2 * slabs,)),
        ],
        vmem_out=True,
    )(
        *(
            pltpu.with_memory_space_constraint(x, pltpu.HBM)
            for x in (predicted, innovation, ensemble, slot_order, taper_level)
        )
    )
    got = exchange(sent)
    own = got.reshape(CHIPS * SENT, LANES)
    slots = got[:: CHIPS // slabs, SLOT_ROW, 0:blocks].astype(jnp.int32)

    part = SHARE * LANES
    first, second = call(turn_kernel, [(CHIPS // 2, part)] * 2, [VMEM])(own)
    x1a = shift(first, 1)
    x1b = shift(second, 1)
    x2b = shift(second, -1)
    x2a = shift(first, -1)
    x3 = shift(x1a, 1)
    x4 = shift(x2b, -1)
    other = swap(own)
    taper, back = call(
        sort_kernel,
        [(regions, data_blocks // 2), (CHIPS * BACK, LANES)],
        [SMEM, VMEM, VMEM, VMEM],
        [
            scratch(data_blocks, regions),
            scratch(regions, data_blocks // 2),
            scratch(regions, data_blocks // 2),
            scratch(regions * HALF, LANES),
        ],
    )(slots, level, own, other)
    near = call(near_kernel, (regions, part), [VMEM] * 7)(
        taper, first, second, x1a, x1b, x2a, x2b
    )
    keep, give = (
        call(functools.partial(far_kernel, rows), (SLAB, part), [VMEM] * 4)(taper, near, x3, x4)
        for rows in (slice(0, SLAB), slice(SLAB, 2 * SLAB))
    )
    back = call(place_kernel, (CHIPS * BACK, LANES), [VMEM] * 3, aliases={2: 0})(
        keep, swap(give), back
    )
    arrived = exchange(back.reshape(CHIPS, BACK, LANES))
    return call(
        update_kernel,
        ensemble.shape,
        [VMEM],
        [
            scratch(members, TILES * LANES),
            scratch(GROUPS * RUN, LANES),
            scratch(members, 2 * LANES),
            pltpu.VMEM((2, members, TILES * LANES), jnp.float32),
            pltpu.SemaphoreType.DMA((2,)),
        ],
        out_spec=HBM,
    )(arrived)


def solution(mesh):
    return jax.shard_map(
        per_device,
        mesh=mesh,
        in_specs=(
            P(None, BOTH),
            P(None, BOTH),
            P(None, BOTH),
            P(),
            P("dp", None),
        ),
        out_specs=P(None, BOTH),
        check_vma=False,
    )
```

```python
import functools

import jax
import jax.numpy as jnp
from jax import lax
from jax.experimental import pallas as pl
from jax.experimental.pallas import tpu as pltpu
from jax.sharding import PartitionSpec as P

LEVELS = 4
LANES = 128
HIGHEST = lax.Precision.HIGHEST
BOTH = ("dp", "region")


def taper_table(levels):
    values = []
    for level in range(levels + 1):
        z = 2.0 * (levels - level) / levels
        if z <= 1.0:
            value = -(z**5) / 4.0 + z**4 / 2.0 + 5.0 * z**3 / 8.0 - 5.0 * z**2 / 3.0 + 1.0
        else:
            value = (
                z**5 / 12.0
                - z**4 / 2.0
                + 5.0 * z**3 / 8.0
                + 5.0 * z**2 / 3.0
                - 5.0 * z
                + 4.0
                - 2.0 / (3.0 * z)
            )
        values.append(max(value, 0.0))
    return values


TABLE = taper_table(LEVELS)

SLAB = 64
CHIPS = 32
SHARE = 10
PIECE = 25
HALF = 32
SENT = 2 * HALF
BACK = 72
TILES = 4
WIDTH = 25
SETS = 5
GROUPS = 8
RUN = 40


def lane_of(rows):
    return lax.broadcasted_iota(jnp.int32, (rows, LANES), 1)


def sent_row(j):
    return j // 5 * HALF + PIECE + j % 5


SLOT_ROW = SENT - 2
NEAR = HALF - PIECE


def back_row(t, j):
    return t * HALF + PIECE + j if j < NEAR else SENT + t * (SHARE - NEAR) + j - NEAR


def pieces():
    count = CHIPS // TILES
    for q in range(CHIPS):
        yield q, q // count, q % count * PIECE


def core_index():
    return lax.rem(lax.axis_index("region"), 2)


def slab_index():
    return lax.div(lax.axis_index("dp"), SLAB // lax.axis_size("region"))


def pack_kernel(
    y_hbm,
    w_hbm,
    ens_hbm,
    slot_hbm,
    level_hbm,
    out_ref,
    level_ref,
    gain,
    packed,
    order,
    y_ref,
    w_ref,
    ens_ref,
    slot_ref,
    sems,
):
    members = ens_ref.shape[0]
    slabs = level_ref.shape[0] // SLAB
    slab = slab_index()
    regions = pl.ds(pl.multiple_of(slab * (2 * SLAB), 2 * SLAB), 2 * SLAB)
    early = [
        pltpu.make_async_copy(ens_hbm, ens_ref, sems.at[0]),
        pltpu.make_async_copy(slot_hbm, slot_ref, sems.at[1]),
    ]
    late = [
        pltpu.make_async_copy(y_hbm, y_ref, sems.at[2]),
        pltpu.make_async_copy(w_hbm, w_ref, sems.at[3]),
    ]
    core = core_index()
    ahead = 1 - 2 * core
    half = SLAB // 2
    for i, by in enumerate((0, slabs - ahead, slabs + ahead, 2)):
        first = lax.rem(slab + by, slabs) * SLAB
        for h in range(2):
            row = pl.multiple_of(first + lax.rem(core + h, 2) * half, half)
            late.append(
                pltpu.make_async_copy(
                    level_hbm.at[pl.ds(row, half), regions],
                    level_ref.at[pl.ds(i * SLAB + h * half, half)],
                    sems.at[4 + 2 * i + h],
                )
            )
    for copy in late[:2] + early + late[2:]:
        copy.start()
    for copy in late[:2]:
        copy.wait()
    gain[:, 0:members] = lax.dot_general(
        w_ref[...], y_ref[...], (((1,), (1,)), ((), ())), preferred_element_type=jnp.float32
    )
    lane = lane_of(RUN)
    for f in range(GROUPS):
        total = None
        for g in range(SETS):
            low = gain[g * RUN : (g + 1) * RUN, 0:LANES]
            high = gain[g * RUN : (g + 1) * RUN, LANES : 2 * LANES]
            start, end = f * WIDTH, (f + 1) * WIDTH
            if end <= LANES:
                part = low
            elif start >= LANES:
                part = high
            else:
                part = jnp.where(lane >= start, low, high)
            part = pltpu.roll(part, (g - f) * WIDTH % LANES, 1)
            total = part if total is None else jnp.where(lane >= g * WIDTH, part, total)
        packed[f * RUN : (f + 1) * RUN, :] = total
    for copy in early + late[2:]:
        copy.wait()
    order[:, 0 : slot_ref.shape[1]] = slot_ref[...].astype(jnp.float32)
    for q, tile, first in pieces():
        for k in range(2):
            column = (k * TILES + tile) * LANES
            out_ref[q, k * HALF : k * HALF + PIECE, :] = ens_ref[
                first : first + PIECE, column : column + LANES
            ]
    for q in range(CHIPS):
        for j in range(0, SHARE, 5):
            out_ref[q, sent_row(j) : sent_row(j) + 5, :] = packed[
                q * SHARE + j : q * SHARE + j + 5, :
            ]
        out_ref[q, SLOT_ROW : SLOT_ROW + 1, :] = order[...]


def turn_kernel(got_ref, first_ref, second_ref):
    core = core_index()
    half = CHIPS // 2
    for j in range(SHARE):
        low = got_ref[pl.ds(sent_row(j), half, stride=SENT), :]
        high = got_ref[pl.ds(half * SENT + sent_row(j), half, stride=SENT), :]
        columns = slice(j * LANES, (j + 1) * LANES)
        first_ref[:, columns] = jnp.where(core == 0, low, high)
        second_ref[:, columns] = jnp.where(core == 0, high, low)


def sort_kernel(
    slot_ref, level_ref, own_ref, other_ref, taper_ref, out_ref, weight, row, ordered, blocks
):
    slabs = slot_ref.shape[0]
    core = core_index()
    levels = level_ref[...]
    total = jnp.zeros(levels.shape, jnp.float32)
    for value in range(LEVELS + 1):
        total = jnp.where(levels == value, jnp.float32(TABLE[value]), total)
    weight[...] = total
    count = levels.shape[0] // 2
    even = weight[pl.ds(0, count, stride=2), :]
    odd = weight[pl.ds(1, count, stride=2), :]
    row[...] = jnp.where(core == 0, even, odd).T
    per = CHIPS // slabs
    for got_ref, side in ((own_ref, core), (other_ref, 1 - core)):
        for k in range(CHIPS):
            for h in range(2):
                region = k % per * 4 + h + 2 * side
                dest = slot_ref[k // per, region] + k // per * 4 * per
                t = lax.bitwise_and(dest, 1)
                away = lax.bitwise_xor(lax.bitwise_and(lax.shift_right_logical(dest, 1), 1), core)
                place = away * SLAB + t * CHIPS + lax.shift_right_logical(dest, 2)
                ordered[pl.ds(place, 1), :] = row[pl.ds(region + k // per * 4 * per, 1), :]
                first = pl.multiple_of(place * HALF, HALF)
                blocks[pl.ds(first, HALF), :] = got_ref[
                    (2 * k + h) * HALF : (2 * k + h + 1) * HALF, :
                ]
    taper_ref[...] = ordered[...]
    for t in range(2):
        for p in range(CHIPS):
            out_ref[p * BACK + t * HALF : p * BACK + (t + 1) * HALF, :] = blocks[
                (t * CHIPS + p) * HALF : (t * CHIPS + p + 1) * HALF, :
            ]


def weigh(taper, x):
    return lax.dot_general(
        taper,
        x,
        (((1,), (0,)), ((), ())),
        precision=HIGHEST,
        preferred_element_type=jnp.float32,
    )


def gain_kernel(rows, taper_ref, *refs):
    x = jnp.concatenate([ref[...] for ref in refs[:-1]], axis=0)
    refs[-1][...] = weigh(taper_ref[rows, :], x)


def place_kernel(keep_ref, taken_ref, back_ref, out_ref):
    del back_ref
    for t in range(2):
        rows = slice(t * CHIPS, (t + 1) * CHIPS)
        for j in range(SHARE):
            columns = slice(j * LANES, (j + 1) * LANES)
            out_ref[pl.ds(back_row(t, j), CHIPS, stride=BACK), :] = (
                keep_ref[rows, columns] + taken_ref[rows, columns]
            )


def update_kernel(got_ref, out_hbm, cells, packed, gain, local_ref, sems):
    members = out_hbm.shape[0]
    wide = TILES * LANES
    copies = [
        pltpu.make_async_copy(
            local_ref.at[t], out_hbm.at[:, pl.ds(t * wide, wide)], sems.at[t]
        )
        for t in range(2)
    ]
    lane = lane_of(RUN)
    for t in range(2):
        for q, tile, first in pieces():
            cells[first : first + PIECE, tile * LANES : (tile + 1) * LANES] = got_ref[
                q, t * HALF : t * HALF + PIECE, :
            ]
            for start, end in ((0, NEAR), (NEAR, SHARE)):
                at = back_row(t, start)
                packed[q * SHARE + start : q * SHARE + end, :] = got_ref[
                    q, at : at + end - start, :
                ]
        for g in range(SETS):
            halves = [None, None]
            for f in range(GROUPS):
                part = pltpu.roll(packed[f * RUN : (f + 1) * RUN, :], (f - g) * WIDTH % LANES, 1)
                for h in range(2):
                    start = f * WIDTH - h * LANES
                    if start < LANES and start + WIDTH > 0:
                        halves[h] = (
                            part if halves[h] is None else jnp.where(lane >= start, part, halves[h])
                        )
            halves[1] = jnp.where(lane < members - LANES, halves[1], 0.0)
            for h in range(2):
                gain[g * RUN : (g + 1) * RUN, h * LANES : (h + 1) * LANES] = halves[h]
        values = cells[...]
        anomaly = values - jnp.mean(values, axis=0, keepdims=True)
        local = lax.dot_general(
            gain[:, 0:members],
            anomaly,
            (((1,), (0,)), ((), ())),
            precision=HIGHEST,
            preferred_element_type=jnp.float32,
        )
        local_ref[t] = local * jnp.float32(1.0 / (members - 1.0))
        copies[t].start()
    for copy in copies:
        copy.wait()


VMEM = pl.BlockSpec(memory_space=pltpu.VMEM)
HBM = pl.BlockSpec(memory_space=pltpu.HBM)
SMEM = pl.BlockSpec(memory_space=pltpu.SMEM)


def call(kernel, shapes, in_specs, scratch=(), aliases=None, out_spec=VMEM, vmem_out=False):
    many = isinstance(shapes, list)
    outs = []
    for shape in shapes if many else [shapes]:
        dims, dtype = shape if isinstance(shape[0], tuple) else (shape, jnp.float32)
        outs.append((pltpu.VMEM if vmem_out else jax.ShapeDtypeStruct)(dims, dtype))
    return pl.pallas_call(
        kernel,
        out_shape=outs if many else outs[0],
        in_specs=in_specs,
        out_specs=[out_spec] * len(outs) if many else out_spec,
        scratch_shapes=list(scratch),
        input_output_aliases=aliases or {},
        compiler_params=pltpu.CompilerParams(vmem_limit_bytes=40 * 1024 * 1024),
    )


def scratch(rows, columns, dtype=jnp.float32):
    return pltpu.VMEM((rows, columns), dtype)


def per_device(ensemble, predicted, innovation, taper_level, slot_order):
    members = ensemble.shape[0]
    blocks = slot_order.shape[1]
    data_blocks = taper_level.shape[0]
    slabs = data_blocks // SLAB
    regions = 2 * SLAB
    groups = [[s * SLAB + 2 * k + c for k in range(CHIPS)] for s in range(slabs) for c in range(2)]

    def shift(x, by):
        pairs = [
            (s * SLAB + a, (s + by * (1 - 2 * (a % 2))) % slabs * SLAB + a)
            for s in range(slabs)
            for a in range(SLAB)
        ]
        return lax.ppermute(x, BOTH, pairs)

    def swap(x):
        return lax.ppermute(x, BOTH, [(i, i ^ 1) for i in range(data_blocks)])

    def exchange(x):
        return lax.all_to_all(
            x, BOTH, split_axis=0, concat_axis=0, tiled=True, axis_index_groups=groups
        )

    sent, level = call(
        pack_kernel,
        [(CHIPS, SENT, LANES), ((data_blocks, regions), jnp.int32)],
        [HBM] * 5,
        [
            scratch(members, 2 * LANES),
            scratch(GROUPS * RUN, LANES),
            scratch(1, LANES),
            scratch(*predicted.shape, predicted.dtype),
            scratch(*innovation.shape, innovation.dtype),
            scratch(*ensemble.shape),
            scratch(*slot_order.shape, slot_order.dtype),
            pltpu.SemaphoreType.DMA((4 + 2 * slabs,)),
        ],
        vmem_out=True,
    )(
        *(
            pltpu.with_memory_space_constraint(x, pltpu.HBM)
            for x in (predicted, innovation, ensemble, slot_order, taper_level)
        )
    )
    got = exchange(sent)
    own = got.reshape(CHIPS * SENT, LANES)
    slots = got[:: CHIPS // slabs, SLOT_ROW, 0:blocks].astype(jnp.int32)

    part = SHARE * LANES
    first, second = call(turn_kernel, [(CHIPS // 2, part)] * 2, [VMEM])(own)
    x1a = shift(first, 1)
    x1b = shift(second, 1)
    x2b = shift(second, -1)
    x2a = shift(first, -1)
    x3 = shift(x1a, 1)
    x4 = shift(x2b, -1)
    other = swap(own)
    taper, back = call(
        sort_kernel,
        [(regions, data_blocks // 2), (CHIPS * BACK, LANES)],
        [SMEM, VMEM, VMEM, VMEM],
        [
            scratch(data_blocks, regions),
            scratch(regions, data_blocks // 2),
            scratch(regions, data_blocks // 2),
            scratch(regions * HALF, LANES),
        ],
    )(slots, level, own, other)
    held = (first, second, x1a, x1b, x2a, x2b, x3, x4)
    keep, give = (
        call(functools.partial(gain_kernel, rows), (SLAB, part), [VMEM] * 9)(taper, *held)
        for rows in (slice(0, SLAB), slice(SLAB, 2 * SLAB))
    )
    back = call(place_kernel, (CHIPS * BACK, LANES), [VMEM] * 3, aliases={2: 0})(
        keep, swap(give), back
    )
    arrived = exchange(back.reshape(CHIPS, BACK, LANES))
    return call(
        update_kernel,
        ensemble.shape,
        [VMEM],
        [
            scratch(members, TILES * LANES),
            scratch(GROUPS * RUN, LANES),
            scratch(members, 2 * LANES),
            pltpu.VMEM((2, members, TILES * LANES), jnp.float32),
            pltpu.SemaphoreType.DMA((2,)),
        ],
        out_spec=HBM,
    )(arrived)


def solution(mesh):
    return jax.shard_map(
        per_device,
        mesh=mesh,
        in_specs=(
            P(None, BOTH),
            P(None, BOTH),
            P(None, BOTH),
            P(),
            P("dp", None),
        ),
        out_specs=P(None, BOTH),
        check_vma=False,
    )
```
